32 devices in a mesh: groups: 2 (over x), gx: 4 (over y, core), gy: 4 (over z).
Axes of the slice: x: 2, y: 2, z: 4, core: 2. Of those that a mesh axis runs over, the one named last changes fastest.
Arguments:
- inputs: bfloat16 [32, 16, 58, 128], P(('groups', 'gx'), 'gy'), parts along dimension 0, may hold values from -6 to 6
- target: bfloat16 [32, 16, 53, 128], P(('groups', 'gx'), 'gy'), parts along dimension 0, may hold values from -6 to 6
- w_first: bfloat16 [3, 3, 3, 58, 64], replicated, may hold values from -0.15625 to 0.15625
- w_second: bfloat16 [3, 3, 3, 64, 53], replicated, may hold values from -0.15625 to 0.15625
Outputs:
- prediction: bfloat16 [32, 16, 53, 128], P(('groups', 'gx'), 'gy'), parts along dimension 0
- grad_first: float32 [6, 3, 3, 58, 64], P('groups'), parts along dimension 0
- grad_second: float32 [6, 3, 3, 64, 53], P('groups'), parts along dimension 0
The draws below stay inside these ranges and needn't reach their ends.
There are 2 independent parts, one for each index of `groups`. The reference program is written for one: setup_inputs(seed, part) draws one part's arguments, and reference() takes and returns one part's arrays. A program takes and returns all parts, laid end to end along the dimension named above; an argument that names none is the same for every part. Nothing has to cross between parts.
All inputs are finite; a program needn't handle non-finite values.
Results may differ from the reference program's by a relative error of at most 0.0049.
Values may be sent and summed in bfloat16 or wider, within the bound.
A program may use at most 64 MiB of HBM per device.

```python
import math
import jax
import jax.numpy as jnp
from jax import lax

CIN = 58
HID = 64
COUT = 53
NZ = 128
NX = 16
NY = 16


def steps_of(own_key, extent, split, smallest, top_value):
    def one(position, blocks):
        heights = jax.random.uniform(jax.random.fold_in(jax.random.fold_in(own_key, 6), position), (blocks,), jnp.float32, smallest / len(split), top_value / len(split))
        return jnp.repeat(jnp.exp(heights), extent[position] // blocks).reshape((-1,) + (1,) * (len(extent) - position - 1))

    loudness = one(*split[0])
    for cut in split[1:]:
        loudness = loudness * one(*cut)
    return loudness


def noise(key, shape, scale, most, split=(), dtype=jnp.bfloat16):
    factor_of = steps_of(key, shape, split, -0.22, 0.18) if split else 1.0
    values = jax.random.normal(key, shape, jnp.float32) * scale * factor_of
    return jnp.minimum(jnp.maximum(values, -most), most).astype(dtype)


def setup_inputs(seed: int = 0, part: int = 0) -> dict:
    key_list = jax.random.split(jax.random.key(seed), 5)
    part_keys = jax.random.split(jax.random.fold_in(key_list[4], part), 5)
    return {
        "inputs": noise(part_keys[0], (NX, NY, CIN, NZ), 1.0, 6.0, ((0, 4), (1, 4))),
        "target": noise(part_keys[1], (NX, NY, COUT, NZ), 1.0, 6.0, ((0, 4), (1, 4))),
        "w_first": noise(key_list[2], (3, 3, 3, CIN, HID), (27 * CIN) ** -0.5, 0.15625),
        "w_second": noise(key_list[3], (3, 3, 3, HID, COUT), (27 * HID) ** -0.5, 0.15625),
    }


root_two_pi = 0.7978845608028654
cubic_term = 0.044715

def smooth_gate(activation):
    tangent = jnp.tanh(root_two_pi * (activation + cubic_term * activation * activation * activation))
    return 0.5 * activation * (1.0 + tangent)

def gate_slope(activation):
    tangent = jnp.tanh(root_two_pi * (activation + cubic_term * activation * activation * activation))
    return 0.5 * (1.0 + tangent) + 0.5 * activation * (1.0 - tangent * tangent) * root_two_pi * (1.0 + 3.0 * cubic_term * activation * activation)

def correlate(field, kernel, padding):
    result = lax.conv_general_dilated(field.astype(jnp.float32)[None], kernel.astype(jnp.float32), (1, 1, 1), padding, dimension_numbers=('NHWCD', 'HWDIO', 'NHWCD'), precision=lax.Precision.HIGHEST, preferred_element_type=jnp.float32)
    return result[0]

def correlate_back(field, kernel, padding):
    flipped = kernel[::-1, ::-1, ::-1].astype(jnp.float32)
    result = lax.conv_general_dilated(field.astype(jnp.float32)[None], flipped, (1, 1, 1), padding, dimension_numbers=('NHWCD', 'HWDOI', 'NHWCD'), precision=lax.Precision.HIGHEST, preferred_element_type=jnp.float32)
    return result[0]

def filter_grad(field, slope_term, padding):
    stacked = lax.conv_general_dilated(field.astype(jnp.float32)[None], slope_term.astype(jnp.float32)[None], (1, 1, 1), padding, dimension_numbers=('CHWND', 'IHWOD', 'NHWCD'), precision=lax.Precision.HIGHEST, preferred_element_type=jnp.float32)
    return jnp.transpose(stacked, (1, 2, 4, 0, 3))

def reference(inputs, target, w_first, w_second):
    whole_pad = [(1, 1), (1, 1), (1, 1)]
    activation = correlate(inputs, w_first, whole_pad)
    hidden = smooth_gate(activation).astype(jnp.bfloat16)
    output = correlate(hidden, w_second, whole_pad)
    prediction = output.astype(jnp.bfloat16)
    normalizer = 1.0 / math.sqrt(NX * NY * NZ)
    output_grad = ((output - target.astype(jnp.float32)) * normalizer).astype(jnp.bfloat16)
    grad_second = filter_grad(hidden, output_grad, whole_pad)
    back_grad = correlate_back(output_grad, w_second, whole_pad)
    slope_term = (back_grad * gate_slope(activation)).astype(jnp.bfloat16)
    grad_first = filter_grad(inputs, slope_term, whole_pad)
    return (prediction, grad_first, grad_second)
```

```python
import functools
import math

import jax
import jax.numpy as jnp
from jax import lax
from jax.experimental import pallas as pl
from jax.experimental.pallas import tpu as pltpu
from jax.sharding import PartitionSpec as P

root_two_pi = 0.7978845608028654
cubic_term = 0.044715
CH = 64
bf16 = jnp.bfloat16
f32 = jnp.float32
DIRECTIONS = ((0, 1), (0, -1), (1, 0), (-1, 0), (1, 1), (1, -1), (-1, 1), (-1, -1))


def kernel(
    nx, ny, bx, by, depth, rows, normalizer,
    x_ref, t_ref, w1_ref, w2_ref, w2b_ref,
    pred_ref, g1_ref, g2_ref,
    raw_in, raw_hid, raw_grad, sh_in, sh_hid, sh_grad, wide_grad, wide_slope,
    act, acc, part, from_x, half, from_y, whole,
    halo_send, halo_recv, x_send, x_recv, y_send, y_recv, ay_send, ay_recv, ax_send, ax_recv,
):
    gx = lax.axis_index("gx")
    gy = lax.axis_index("gy")
    lanes = bx * depth
    wide = lanes + 2 * depth
    inner = slice(depth, depth + lanes)

    raw_in[...] = jnp.zeros_like(raw_in)
    raw_hid[...] = jnp.zeros_like(raw_hid)
    raw_grad[...] = jnp.zeros_like(raw_grad)
    raw_in[1 : by + 1, :, inner] = x_ref[...]

    barrier = pltpu.get_barrier_semaphore()
    for dx in range(nx):
        for dy in range(ny):
            if dx or dy:
                pl.semaphore_signal(
                    barrier,
                    inc=1,
                    device_id={"gx": lax.rem(gx + dx, nx), "gy": lax.rem(gy + dy, ny)},
                    device_id_type=pl.DeviceIdType.MESH,
                )
    pl.semaphore_wait(barrier, nx * ny - 1)

    def spans(step, count, unit):
        source = {0: (1, count), 1: (count, 1), -1: (1, 1)}[step]
        target = {0: (1, count), 1: (0, 1), -1: (count + 1, 1)}[step]
        return (
            slice(source[0] * unit, (source[0] + source[1]) * unit),
            slice(target[0] * unit, (target[0] + target[1]) * unit),
        )

    def halo(raw, slot):
        result = []
        for index, (dx, dy) in enumerate(DIRECTIONS):
            x_source, x_target = spans(dx, bx, depth)
            y_source, y_target = spans(dy, by, 1)
            to_x, to_y = gx + dx, gy + dy
            from_x_, from_y_ = gx - dx, gy - dy
            sends = (to_x >= 0) & (to_x < nx) & (to_y >= 0) & (to_y < ny)
            receives = (from_x_ >= 0) & (from_x_ < nx) & (from_y_ >= 0) & (from_y_ < ny)
            copy = pltpu.make_async_remote_copy(
                src_ref=raw.at[y_source, :, x_source],
                dst_ref=raw.at[y_target, :, x_target],
                send_sem=halo_send.at[slot, index],
                recv_sem=halo_recv.at[slot, index],
                device_id={"gx": lax.rem(to_x + nx, nx), "gy": lax.rem(to_y + ny, ny)},
                device_id_type=pl.DeviceIdType.MESH,
            )
            result.append((sends, receives, copy))
        return result

    def start(copies):
        for sends, _, copy in copies:
            pl.when(sends)(copy.start)

    def arrive(copies):
        for _, receives, copy in copies:
            pl.when(receives)(copy.wait_recv)

    def leave(copies):
        for sends, _, copy in copies:
            pl.when(sends)(copy.wait_send)

    place = lax.rem(lax.broadcasted_iota(jnp.int32, (CH, wide), 1), depth)
    first = place == 0
    last = place == depth - 1

    def shift(raw, out):
        def body(y, _):
            value = raw[y]
            out[y, CH : 2 * CH, :] = value
            full = value.astype(f32)
            out[y, :CH, :] = jnp.where(first, 0.0, pltpu.roll(full, 1, 1)).astype(bf16)
            out[y, 2 * CH :, :] = jnp.where(last, 0.0, pltpu.roll(full, wide - 1, 1)).astype(bf16)
            return 0

        lax.fori_loop(0, by + 2, body, 0)

    def conv(field, weight, y):
        block = field[pl.ds(y, 3)].reshape(9 * CH, wide)
        taps = jnp.dot(weight[...], block, preferred_element_type=f32)
        return (
            taps[:CH, :lanes]
            + taps[CH : 2 * CH, depth : depth + lanes]
            + taps[2 * CH :, 2 * depth :]
        )

    def spread(out, y, value):
        for a in range(3):
            if a:
                out[y, a * CH : (a + 1) * CH, : a * depth] = jnp.zeros((CH, a * depth), bf16)
            if a < 2:
                out[y, a * CH : (a + 1) * CH, a * depth + lanes :] = jnp.zeros(
                    (CH, (2 - a) * depth), bf16
                )
            out[y, a * CH : (a + 1) * CH, a * depth : a * depth + lanes] = value

    def filter_grad(field, terms, slot):
        acc[...] = jnp.zeros_like(acc)

        def body(y, _):
            block = field[pl.ds(y, 3)].reshape(9 * CH, wide)
            acc[...] += lax.dot_general(
                block, terms[y], (((1,), (1,)), ((), ())), preferred_element_type=f32
            )
            return 0

        lax.fori_loop(0, by, body, 0)
        used = 9 * CH
        mid = used // 2
        part[slot, :used, :] = acc[:, : 2 * CH].astype(bf16)
        part[slot, used : used + mid, :] = jnp.concatenate(
            [acc[:mid, 2 * CH :], acc[mid:, 2 * CH :]], axis=1
        ).astype(bf16)
        total = nx * ny * rows
        if total > used + mid:
            part[slot, used + mid :, :] = jnp.zeros((total - used - mid, 2 * CH), bf16)

    def remote(src, dst, send, recv, device):
        return pltpu.make_async_remote_copy(
            src_ref=src, dst_ref=dst, send_sem=send, recv_sem=recv,
            device_id=device, device_id_type=pl.DeviceIdType.MESH,
        )

    def span_x(index):
        return pl.ds(pl.multiple_of(index * (ny * rows), 16), ny * rows)

    def span_y(index):
        return pl.ds(pl.multiple_of(index * rows, 16), rows)

    def span_own():
        return pl.ds(pl.multiple_of((gx * ny + gy) * rows, 16), rows)

    def scatter_x(slot):
        copies = []
        for d in range(1, nx):
            to = lax.rem(gx + d, nx)
            copies.append(remote(
                part.at[slot, span_x(to)], from_x.at[slot, d - 1],
                x_send.at[slot, d - 1], x_recv.at[slot, d - 1], {"gx": to},
            ))
            copies[-1].start()
        return copies

    def scatter_y(slot, copies):
        total = part[slot, span_x(gx)].astype(f32)
        for d, copy in enumerate(copies):
            copy.wait_recv()
            total = total + from_x[slot, d].astype(f32)
        half[slot] = total.astype(bf16)
        result = []
        for d in range(1, ny):
            to = lax.rem(gy + d, ny)
            result.append(remote(
                half.at[slot, span_y(to)], from_y.at[slot, d - 1],
                y_send.at[slot, d - 1], y_recv.at[slot, d - 1], {"gy": to},
            ))
            result[-1].start()
        return result

    def gather_y(slot, copies):
        total = half[slot, span_y(gy)].astype(f32)
        for d, copy in enumerate(copies):
            copy.wait_recv()
            total = total + from_y[slot, d].astype(f32)
        whole[slot, span_own()] = total.astype(bf16)
        result = []
        for d in range(1, ny):
            to = lax.rem(gy + d, ny)
            result.append(remote(
                whole.at[slot, span_own()], whole.at[slot, span_own()],
                ay_send.at[slot, d - 1], ay_recv.at[slot, d - 1], {"gy": to},
            ))
            result[-1].start()
        return result

    def gather_x(slot, copies):
        for copy in copies:
            copy.wait_recv()
        result = []
        for d in range(1, nx):
            to = lax.rem(gx + d, nx)
            result.append(remote(
                whole.at[slot, span_x(gx)], whole.at[slot, span_x(gx)],
                ax_send.at[slot, d - 1], ax_recv.at[slot, d - 1], {"gx": to},
            ))
            result[-1].start()
        return result

    def finish(slot, copies, out):
        for copy in copies:
            copy.wait_recv()
        used = 9 * CH
        mid = used // 2
        both = whole[slot, :used, :].astype(f32)
        out[0] = both[:, :CH]
        out[1] = both[:, CH:]
        rest = whole[slot, used : used + mid, :].astype(f32)
        out[2, :mid, :] = rest[:, :CH]
        out[2, mid:, :] = rest[:, CH:]

    in_copies = halo(raw_in, 0)
    start(in_copies)
    arrive(in_copies)
    shift(raw_in, sh_in)

    def first_layer(y, _):
        value = conv(sh_in, w1_ref, y)
        act[y] = value
        tangent = jnp.tanh(root_two_pi * (value + cubic_term * value * value * value))
        raw_hid[y + 1, :, inner] = (0.5 * value * (1.0 + tangent)).astype(bf16)
        return 0

    lax.fori_loop(0, by, first_layer, 0)
    hid_copies = halo(raw_hid, 1)
    start(hid_copies)

    def slopes(y, _):
        value = act[y]
        tangent = jnp.tanh(root_two_pi * (value + cubic_term * value * value * value))
        act[y] = 0.5 * (1.0 + tangent) + 0.5 * value * (
            1.0 - tangent * tangent
        ) * root_two_pi * (1.0 + 3.0 * cubic_term * value * value)
        return 0

    lax.fori_loop(0, by, slopes, 0)
    arrive(hid_copies)
    shift(raw_hid, sh_hid)

    def second_layer(y, _):
        value = conv(sh_hid, w2_ref, y)
        pred_ref[y] = value.astype(bf16)
        grad = ((value - t_ref[y].astype(f32)) * normalizer).astype(bf16)
        raw_grad[y + 1, :, inner] = grad
        spread(wide_grad, y, grad)
        return 0

    lax.fori_loop(0, by, second_layer, 0)
    grad_copies = halo(raw_grad, 2)
    start(grad_copies)
    filter_grad(sh_hid, wide_grad, 1)
    scatter_x_second = scatter_x(1)
    arrive(grad_copies)
    shift(raw_grad, sh_grad)

    def back(y, _):
        value = conv(sh_grad, w2b_ref, y)
        spread(wide_slope, y, (value * act[y]).astype(bf16))
        return 0

    lax.fori_loop(0, by, back, 0)
    scatter_y_second = scatter_y(1, scatter_x_second)
    filter_grad(sh_in, wide_slope, 0)
    scatter_x_first = scatter_x(0)
    gather_y_second = gather_y(1, scatter_y_second)
    scatter_y_first = scatter_y(0, scatter_x_first)
    gather_x_second = gather_x(1, gather_y_second)
    gather_y_first = gather_y(0, scatter_y_first)
    finish(1, gather_x_second, g2_ref)
    gather_x_first = gather_x(0, gather_y_first)
    finish(0, gather_x_first, g1_ref)

    for copies in (in_copies, hid_copies, grad_copies):
        leave(copies)
    for copies in (
        scatter_x_second, scatter_y_second, gather_y_second, gather_x_second,
        scatter_x_first, scatter_y_first, gather_y_first, gather_x_first,
    ):
        for copy in copies:
            copy.wait_send()


def on_device(nx, ny, inputs, target, w_first, w_second):
    bx, by, cin, depth = inputs.shape
    cout = target.shape[2]
    hid = w_first.shape[4]
    normalizer = 1.0 / math.sqrt(bx * nx * by * ny * depth)
    used = 9 * CH * 3 // 2
    rows = -(-used // (nx * ny * 16)) * 16

    def flat(field):
        padded = jnp.pad(field, ((0, 0), (0, 0), (0, CH - field.shape[2]), (0, 0)))
        return padded.transpose(1, 2, 0, 3).reshape(by, CH, bx * depth)

    def weights(w, order):
        w = jnp.pad(w, ((0, 0),) * 3 + ((0, CH - w.shape[3]), (0, CH - w.shape[4])))
        return w.transpose(order).reshape(3 * CH, 9 * CH)

    forward = (0, 4, 1, 2, 3)
    lanes = bx * depth
    wide = lanes + 2 * depth
    vmem = pl.BlockSpec(memory_space=pltpu.VMEM)
    total = nx * ny * rows
    dma = pltpu.SemaphoreType.DMA
    macs = 5 * 192 * 576 * wide * by
    prediction, g1, g2 = pl.pallas_call(
        functools.partial(kernel, nx, ny, bx, by, depth, rows, normalizer),
        out_shape=(
            jax.ShapeDtypeStruct((by, CH, lanes), bf16),
            jax.ShapeDtypeStruct((3, 9 * CH, CH), f32),
            jax.ShapeDtypeStruct((3, 9 * CH, CH), f32),
        ),
        in_specs=[vmem] * 5,
        out_specs=(vmem,) * 3,
        scratch_shapes=(
            [pltpu.VMEM((by + 2, CH, wide), bf16)] * 3
            + [pltpu.VMEM((by + 2, 3 * CH, wide), bf16)] * 3
            + [pltpu.VMEM((by, 3 * CH, wide), bf16)] * 2
            + [
                pltpu.VMEM((by, CH, lanes), f32),
                pltpu.VMEM((9 * CH, 3 * CH), f32),
                pltpu.VMEM((2, total, 2 * CH), bf16),
                pltpu.VMEM((2, nx - 1, ny * rows, 2 * CH), bf16),
                pltpu.VMEM((2, ny * rows, 2 * CH), bf16),
                pltpu.VMEM((2, ny - 1, rows, 2 * CH), bf16),
                pltpu.VMEM((2, total, 2 * CH), bf16),
                dma((3, 8)), dma((3, 8)),
                dma((2, nx - 1)), dma((2, nx - 1)),
                dma((2, ny - 1)), dma((2, ny - 1)),
                dma((2, ny - 1)), dma((2, ny - 1)),
                dma((2, nx - 1)), dma((2, nx - 1)),
            ]
        ),
        compiler_params=pltpu.CompilerParams(
            collective_id=0, has_side_effects=True, vmem_limit_bytes=48 * 1024 * 1024
        ),
        cost_estimate=pl.CostEstimate(
            flops=2 * macs, bytes_accessed=8 * 2**20, transcendentals=2 * by * CH * lanes
        ),
    )(
        flat(inputs),
        flat(target),
        weights(w_first, forward),
        weights(w_second, forward),
        weights(w_second[::-1, ::-1, ::-1], (0, 3, 1, 2, 4)),
    )
    prediction = prediction.reshape(by, CH, bx, depth).transpose(2, 0, 1, 3)[:, :, :cout]
    g1 = g1.reshape(3, 3, 3, CH, CH)[:, :, :, :cin, :hid]
    g2 = g2.reshape(3, 3, 3, CH, CH)[:, :, :, :hid, :cout]
    return prediction, g1, g2


def solution(mesh):
    placed = (
        P(("groups", "gx"), "gy", None, None),
        P(("groups", "gx"), "gy", None, None),
        P(),
        P(),
    )
    return jax.shard_map(
        functools.partial(on_device, mesh.shape["gx"], mesh.shape["gy"]),
        mesh=mesh,
        in_specs=placed,
        out_specs=(
            P(("groups", "gx"), "gy", None, None),
            P("groups", None, None, None, None),
            P("groups", None, None, None, None),
        ),
        check_vma=False,
    )
```

```python
import functools
import math

import jax
import jax.numpy as jnp
from jax import lax
from jax.experimental import pallas as pl
from jax.experimental.pallas import tpu as pltpu
from jax.sharding import PartitionSpec as P

root_two_pi = 0.7978845608028654
cubic_term = 0.044715
CH = 64
bf16 = jnp.bfloat16
f32 = jnp.float32
DIRECTIONS = ((0, 1), (0, -1), (1, 0), (-1, 0), (1, 1), (1, -1), (-1, 1), (-1, -1))


def kernel(
    nx, ny, bx, by, depth, rows, normalizer,
    x_ref, t_ref, w1_ref, w2_ref,
    pred_ref, g1_ref, g2_ref,
    raw_in, raw_hid, raw_grad, sh_in, sh_hid, sh_grad, wide_grad, wide_slope,
    first_w, second_w, back_w, act, acc, part, from_x, half, from_y, whole,
    halo_send, halo_recv, x_send, x_recv, y_send, y_recv, ay_send, ay_recv, ax_send, ax_recv,
):
    gx = lax.axis_index("gx")
    gy = lax.axis_index("gy")
    lanes = by * depth
    wide = lanes + 2 * depth
    inner = slice(depth, depth + lanes)

    for raw in (raw_in, raw_hid, raw_grad):
        raw[0] = jnp.zeros((CH, wide), bf16)
        raw[bx + 1] = jnp.zeros((CH, wide), bf16)
        raw[1 : bx + 1, :, :depth] = jnp.zeros((bx, CH, depth), bf16)
        raw[1 : bx + 1, :, depth + lanes :] = jnp.zeros((bx, CH, depth), bf16)
    raw_in[1 : bx + 1, :, inner] = x_ref[...]

    barrier = pltpu.get_barrier_semaphore()
    for dx in range(nx):
        for dy in range(ny):
            if dx or dy:
                pl.semaphore_signal(
                    barrier,
                    inc=1,
                    device_id={"gx": lax.rem(gx + dx, nx), "gy": lax.rem(gy + dy, ny)},
                    device_id_type=pl.DeviceIdType.MESH,
                )
    pl.semaphore_wait(barrier, nx * ny - 1)

    def spans(step, count, unit):
        source = {0: (1, count), 1: (count, 1), -1: (1, 1)}[step]
        target = {0: (1, count), 1: (0, 1), -1: (count + 1, 1)}[step]
        return (
            slice(source[0] * unit, (source[0] + source[1]) * unit),
            slice(target[0] * unit, (target[0] + target[1]) * unit),
        )

    def halo(raw, slot):
        result = []
        for index, (dx, dy) in enumerate(DIRECTIONS):
            x_source, x_target = spans(dx, bx, 1)
            y_source, y_target = spans(dy, by, depth)
            to_x, to_y = gx + dx, gy + dy
            from_x_, from_y_ = gx - dx, gy - dy
            sends = (to_x >= 0) & (to_x < nx) & (to_y >= 0) & (to_y < ny)
            receives = (from_x_ >= 0) & (from_x_ < nx) & (from_y_ >= 0) & (from_y_ < ny)
            copy = pltpu.make_async_remote_copy(
                src_ref=raw.at[x_source, :, y_source],
                dst_ref=raw.at[x_target, :, y_target],
                send_sem=halo_send.at[slot, index],
                recv_sem=halo_recv.at[slot, index],
                device_id={"gx": lax.rem(to_x + nx, nx), "gy": lax.rem(to_y + ny, ny)},
                device_id_type=pl.DeviceIdType.MESH,
            )
            result.append((sends, receives, copy))
        return result

    def start(copies):
        for sends, _, copy in copies:
            pl.when(sends)(copy.start)

    def arrive(copies):
        for _, receives, copy in copies:
            pl.when(receives)(copy.wait_recv)

    def leave(copies):
        for sends, _, copy in copies:
            pl.when(sends)(copy.wait_send)

    place = lax.rem(lax.broadcasted_iota(jnp.int32, (CH, wide), 1), depth)
    first = place == 0
    last = place == depth - 1

    def shift(raw, out):
        def body(x, _):
            value = raw[x]
            out[x, CH : 2 * CH, :] = value
            full = value.astype(f32)
            out[x, :CH, :] = jnp.where(first, 0.0, pltpu.roll(full, 1, 1)).astype(bf16)
            out[x, 2 * CH :, :] = jnp.where(last, 0.0, pltpu.roll(full, wide - 1, 1)).astype(bf16)
            return 0

        lax.fori_loop(0, bx + 2, body, 0)

    def conv(field, weight, x):
        block = field[pl.ds(x, 3)].reshape(9 * CH, wide)
        taps = jnp.dot(weight[...], block, preferred_element_type=f32)
        return (
            taps[:CH, :lanes]
            + taps[CH : 2 * CH, depth : depth + lanes]
            + taps[2 * CH :, 2 * depth :]
        )

    def spread(out, x, value):
        for a in range(3):
            if a:
                out[x, a * CH : (a + 1) * CH, : a * depth] = jnp.zeros((CH, a * depth), bf16)
            if a < 2:
                out[x, a * CH : (a + 1) * CH, a * depth + lanes :] = jnp.zeros(
                    (CH, (2 - a) * depth), bf16
                )
            out[x, a * CH : (a + 1) * CH, a * depth : a * depth + lanes] = value

    def filter_grad(field, terms, slot):
        acc[...] = jnp.zeros_like(acc)

        def body(x, _):
            block = field[pl.ds(x, 3)].reshape(9 * CH, wide)
            acc[...] += lax.dot_general(
                block, terms[x], (((1,), (1,)), ((), ())), preferred_element_type=f32
            )
            return 0

        lax.fori_loop(0, bx, body, 0)
        used = 9 * CH
        mid = used // 2
        part[slot, :used, :] = acc[:, : 2 * CH].astype(bf16)
        part[slot, used : used + mid, :] = jnp.concatenate(
            [acc[:mid, 2 * CH :], acc[mid:, 2 * CH :]], axis=1
        ).astype(bf16)
        total = nx * ny * rows
        if total > used + mid:
            part[slot, used + mid :, :] = jnp.zeros((total - used - mid, 2 * CH), bf16)

    def remote(src, dst, send, recv, device):
        return pltpu.make_async_remote_copy(
            src_ref=src, dst_ref=dst, send_sem=send, recv_sem=recv,
            device_id=device, device_id_type=pl.DeviceIdType.MESH,
        )

    def span_x(index):
        return pl.ds(pl.multiple_of(index * (ny * rows), 16), ny * rows)

    def span_y(index):
        return pl.ds(pl.multiple_of(index * rows, 16), rows)

    def span_own():
        return pl.ds(pl.multiple_of((gx * ny + gy) * rows, 16), rows)

    def scatter_x(slot):
        copies = []
        for d in range(1, nx):
            to = lax.rem(gx + d, nx)
            copies.append(remote(
                part.at[slot, span_x(to)], from_x.at[slot, d - 1],
                x_send.at[slot, d - 1], x_recv.at[slot, d - 1], {"gx": to},
            ))
            copies[-1].start()
        return copies

    def scatter_y(slot, copies):
        total = part[slot, span_x(gx)].astype(f32)
        for d, copy in enumerate(copies):
            copy.wait_recv()
            total = total + from_x[slot, d].astype(f32)
        half[slot] = total.astype(bf16)
        result = []
        for d in range(1, ny):
            to = lax.rem(gy + d, ny)
            result.append(remote(
                half.at[slot, span_y(to)], from_y.at[slot, d - 1],
                y_send.at[slot, d - 1], y_recv.at[slot, d - 1], {"gy": to},
            ))
            result[-1].start()
        return result

    def gather_y(slot, copies):
        total = half[slot, span_y(gy)].astype(f32)
        for d, copy in enumerate(copies):
            copy.wait_recv()
            total = total + from_y[slot, d].astype(f32)
        whole[slot, span_own()] = total.astype(bf16)
        result = []
        for d in range(1, ny):
            to = lax.rem(gy + d, ny)
            result.append(remote(
                whole.at[slot, span_own()], whole.at[slot, span_own()],
                ay_send.at[slot, d - 1], ay_recv.at[slot, d - 1], {"gy": to},
            ))
            result[-1].start()
        return result

    def gather_x(slot, copies):
        for copy in copies:
            copy.wait_recv()
        result = []
        for d in range(1, nx):
            to = lax.rem(gx + d, nx)
            result.append(remote(
                whole.at[slot, span_x(gx)], whole.at[slot, span_x(gx)],
                ax_send.at[slot, d - 1], ax_recv.at[slot, d - 1], {"gx": to},
            ))
            result[-1].start()
        return result

    def finish(slot, copies, out):
        for copy in copies:
            copy.wait_recv()
        used = 9 * CH
        mid = used // 2
        both = whole[slot, :used, :].astype(f32)
        rest = whole[slot, used : used + mid, :].astype(f32)
        rest = jnp.concatenate([rest[:, :CH], rest[:, CH:]], axis=0)
        third = 3 * CH
        for a in range(3):
            out[a, 0] = both[a * third : (a + 1) * third, :CH]
            out[a, 1] = both[a * third : (a + 1) * third, CH:]
            out[a, 2] = rest[a * third : (a + 1) * third]

    def turned(blocks):
        stacked = jnp.concatenate([block.astype(f32) for block in blocks], axis=0)
        return stacked.T.astype(bf16)

    in_copies = halo(raw_in, 0)
    start(in_copies)
    for b in range(3):
        first_w[b * CH : (b + 1) * CH, :] = turned(
            [w1_ref[(a * 3 + b) * 3 + c] for a in range(3) for c in range(3)]
        )
        for a in range(3):
            for c in range(3):
                column = (a * 3 + c) * CH
                second_w[b * CH : (b + 1) * CH, column : column + CH] = w2_ref[(a * 3 + b) * 3 + c]
    arrive(in_copies)
    shift(raw_in, sh_in)

    def first_layer(x, _):
        value = conv(sh_in, first_w, x)
        act[x] = value
        tangent = jnp.tanh(root_two_pi * (value + cubic_term * value * value * value))
        raw_hid[x + 1, :, inner] = (0.5 * value * (1.0 + tangent)).astype(bf16)
        return 0

    lax.fori_loop(0, bx, first_layer, 0)
    hid_copies = halo(raw_hid, 1)
    start(hid_copies)
    for b in range(3):
        back_w[b * CH : (b + 1) * CH, :] = turned(
            [w2_ref[((2 - a) * 3 + 2 - b) * 3 + 2 - c] for a in range(3) for c in range(3)]
        )

    def slopes(x, _):
        value = act[x]
        tangent = jnp.tanh(root_two_pi * (value + cubic_term * value * value * value))
        act[x] = 0.5 * (1.0 + tangent) + 0.5 * value * (
            1.0 - tangent * tangent
        ) * root_two_pi * (1.0 + 3.0 * cubic_term * value * value)
        return 0

    lax.fori_loop(0, bx, slopes, 0)
    arrive(hid_copies)
    shift(raw_hid, sh_hid)

    def second_layer(x, _):
        value = conv(sh_hid, second_w, x)
        pred_ref[x] = value.astype(bf16)
        grad = ((value - t_ref[x].astype(f32)) * normalizer).astype(bf16)
        raw_grad[x + 1, :, inner] = grad
        spread(wide_grad, x, grad)
        return 0

    lax.fori_loop(0, bx, second_layer, 0)
    grad_copies = halo(raw_grad, 2)
    start(grad_copies)
    filter_grad(sh_hid, wide_grad, 1)
    scatter_x_second = scatter_x(1)
    arrive(grad_copies)
    shift(raw_grad, sh_grad)

    def back(x, _):
        value = conv(sh_grad, back_w, x)
        spread(wide_slope, x, (value * act[x]).astype(bf16))
        return 0

    lax.fori_loop(0, bx, back, 0)
    scatter_y_second = scatter_y(1, scatter_x_second)
    filter_grad(sh_in, wide_slope, 0)
    scatter_x_first = scatter_x(0)
    gather_y_second = gather_y(1, scatter_y_second)
    scatter_y_first = scatter_y(0, scatter_x_first)
    gather_x_second = gather_x(1, gather_y_second)
    gather_y_first = gather_y(0, scatter_y_first)
    finish(1, gather_x_second, g2_ref)
    gather_x_first = gather_x(0, gather_y_first)
    finish(0, gather_x_first, g1_ref)

    for copies in (in_copies, hid_copies, grad_copies):
        leave(copies)
    for copies in (
        scatter_x_second, scatter_y_second, gather_y_second, gather_x_second,
        scatter_x_first, scatter_y_first, gather_y_first, gather_x_first,
    ):
        for copy in copies:
            copy.wait_send()


def on_device(nx, ny, inputs, target, w_first, w_second):
    bx, by, cin, depth = inputs.shape
    cout = target.shape[2]
    hid = w_first.shape[4]
    normalizer = 1.0 / math.sqrt(bx * nx * by * ny * depth)
    used = 9 * CH * 3 // 2
    rows = -(-used // (nx * ny * 16)) * 16

    def flat(field):
        rolled = field.transpose(0, 2, 1, 3).reshape(bx, field.shape[2], by * depth)
        return jnp.pad(rolled, ((0, 0), (0, CH - field.shape[2]), (0, 0)))

    def taps(w):
        w = jnp.pad(w, ((0, 0),) * 3 + ((0, CH - w.shape[3]), (0, CH - w.shape[4])))
        return w.reshape(27, CH, CH)

    lanes = by * depth
    wide = lanes + 2 * depth
    vmem = pl.BlockSpec(memory_space=pltpu.VMEM)
    total = nx * ny * rows
    dma = pltpu.SemaphoreType.DMA
    macs = 5 * 192 * 576 * wide * bx
    prediction, g1, g2 = pl.pallas_call(
        functools.partial(kernel, nx, ny, bx, by, depth, rows, normalizer),
        out_shape=(
            jax.ShapeDtypeStruct((bx, CH, lanes), bf16),
            jax.ShapeDtypeStruct((3, 3, 3 * CH, CH), f32),
            jax.ShapeDtypeStruct((3, 3, 3 * CH, CH), f32),
        ),
        in_specs=[vmem] * 4,
        out_specs=(vmem,) * 3,
        scratch_shapes=(
            [pltpu.VMEM((bx + 2, CH, wide), bf16)] * 3
            + [pltpu.VMEM((bx + 2, 3 * CH, wide), bf16)] * 3
            + [pltpu.VMEM((bx, 3 * CH, wide), bf16)] * 2
            + [pltpu.VMEM((3 * CH, 9 * CH), bf16)] * 3
            + [
                pltpu.VMEM((bx, CH, lanes), f32),
                pltpu.VMEM((9 * CH, 3 * CH), f32),
                pltpu.VMEM((2, total, 2 * CH), bf16),
                pltpu.VMEM((2, nx - 1, ny * rows, 2 * CH), bf16),
                pltpu.VMEM((2, ny * rows, 2 * CH), bf16),
                pltpu.VMEM((2, ny - 1, rows, 2 * CH), bf16),
                pltpu.VMEM((2, total, 2 * CH), bf16),
                dma((3, 8)), dma((3, 8)),
                dma((2, nx - 1)), dma((2, nx - 1)),
                dma((2, ny - 1)), dma((2, ny - 1)),
                dma((2, ny - 1)), dma((2, ny - 1)),
                dma((2, nx - 1)), dma((2, nx - 1)),
            ]
        ),
        compiler_params=pltpu.CompilerParams(
            collective_id=0, has_side_effects=True, vmem_limit_bytes=48 * 1024 * 1024
        ),
        cost_estimate=pl.CostEstimate(
            flops=2 * macs, bytes_accessed=8 * 2**20, transcendentals=2 * bx * CH * lanes
        ),
    )(
        flat(inputs),
        flat(target),
        taps(w_first),
        taps(w_second.transpose(0, 1, 2, 4, 3)),
    )
    prediction = prediction.reshape(bx, CH, by, depth)[:, :cout].transpose(0, 2, 1, 3)
    g1 = g1.reshape(3, 3, 3, CH, CH)[:, :, :, :cin, :hid]
    g2 = g2.reshape(3, 3, 3, CH, CH)[:, :, :, :hid, :cout]
    return prediction, g1, g2


def solution(mesh):
    placed = (
        P(("groups", "gx"), "gy", None, None),
        P(("groups", "gx"), "gy", None, None),
        P(),
        P(),
    )
    return jax.shard_map(
        functools.partial(on_device, mesh.shape["gx"], mesh.shape["gy"]),
        mesh=mesh,
        in_specs=placed,
        out_specs=(
            P(("groups", "gx"), "gy", None, None),
            P("groups", None, None, None, None),
            P("groups", None, None, None, None),
        ),
        check_vma=False,
    )
```

```python
import functools
import math

import jax
import jax.numpy as jnp
from jax import lax
from jax.experimental import pallas as pl
from jax.experimental.pallas import tpu as pltpu
from jax.sharding import PartitionSpec as P

root_two_pi = 0.7978845608028654
cubic_term = 0.044715
CH = 64
bf16 = jnp.bfloat16
f32 = jnp.float32
DIRECTIONS = ((0, 1), (0, -1), (1, 0), (-1, 0), (1, 1), (1, -1), (-1, 1), (-1, -1))


def kernel(
    nx, ny, bx, by, depth, rows, normalizer,
    x_ref, t_ref, w1_hbm, w2_hbm,
    pred_ref, g1_ref, g2_ref,
    raw_in, raw_hid, raw_grad, sh_in, sh_hid, sh_grad, wide_grad, wide_slope,
    w1_ref, w2_ref, w_sem, first_w, second_w, back_w, act, acc, part, from_x, half, from_y, whole,
    halo_send, halo_recv, x_send, x_recv, y_send, y_recv, ay_send, ay_recv, ax_send, ax_recv,
):
    gx = lax.axis_index("gx")
    gy = lax.axis_index("gy")
    lanes = by * depth
    wide = lanes + 2 * depth
    inner = slice(depth, depth + lanes)

    loads = [
        pltpu.make_async_copy(w1_hbm, w1_ref, w_sem.at[0]),
        pltpu.make_async_copy(w2_hbm, w2_ref, w_sem.at[1]),
    ]
    for load in loads:
        load.start()
    for raw in (raw_in, raw_hid, raw_grad):
        raw[0] = jnp.zeros((CH, wide), bf16)
        raw[bx + 1] = jnp.zeros((CH, wide), bf16)
        raw[1 : bx + 1, :, :depth] = jnp.zeros((bx, CH, depth), bf16)
        raw[1 : bx + 1, :, depth + lanes :] = jnp.zeros((bx, CH, depth), bf16)
    raw_in[1 : bx + 1, :, inner] = x_ref[...]

    barrier = pltpu.get_barrier_semaphore()
    def filled(block):
        missing = CH - block.shape[0]
        return jnp.concatenate([block.astype(f32), jnp.zeros((missing, CH), f32)], axis=0)

    def turned(blocks):
        stacked = jnp.concatenate([filled(block) for block in blocks], axis=0)
        return stacked.T.astype(bf16)

    def prepare():
        for load in loads:
            load.wait()
        for b in range(3):
            first_w[b * CH : (b + 1) * CH, :] = turned(
                [w1_ref[(a * 3 + b) * 3 + c] for a in range(3) for c in range(3)]
            )
            for a in range(3):
                for c in range(3):
                    column = (a * 3 + c) * CH
                    second_w[b * CH : (b + 1) * CH, column : column + CH] = filled(
                        w2_ref[(a * 3 + b) * 3 + c]
                    ).astype(bf16)

    def greet(x, y):
        pl.semaphore_signal(
            barrier, inc=1, device_id={"gx": x, "gy": y}, device_id_type=pl.DeviceIdType.MESH
        )

    for dx, dy in DIRECTIONS[4:]:
        x, y = gx + dx, gy + dy
        pl.when((x >= 0) & (x < nx) & (y >= 0) & (y < ny))(
            functools.partial(greet, lax.rem(x + nx, nx), lax.rem(y + ny, ny))
        )
    for d in range(1, nx):
        greet(lax.rem(gx + d, nx), gy)
    for d in range(1, ny):
        greet(gx, lax.rem(gy + d, ny))
    beside_x = lax.div(gx + nx - 1, nx) + lax.div(2 * nx - 2 - gx, nx)
    beside_y = lax.div(gy + ny - 1, ny) + lax.div(2 * ny - 2 - gy, ny)
    pl.semaphore_wait(barrier, nx + ny - 2 + beside_x * beside_y)

    def spans(step, count, unit):
        source = {0: (1, count), 1: (count, 1), -1: (1, 1)}[step]
        target = {0: (1, count), 1: (0, 1), -1: (count + 1, 1)}[step]
        return (
            slice(source[0] * unit, (source[0] + source[1]) * unit),
            slice(target[0] * unit, (target[0] + target[1]) * unit),
        )

    def halo(raw, slot):
        result = []
        for index, (dx, dy) in enumerate(DIRECTIONS):
            x_source, x_target = spans(dx, bx, 1)
            y_source, y_target = spans(dy, by, depth)
            to_x, to_y = gx + dx, gy + dy
            from_x_, from_y_ = gx - dx, gy - dy
            sends = (to_x >= 0) & (to_x < nx) & (to_y >= 0) & (to_y < ny)
            receives = (from_x_ >= 0) & (from_x_ < nx) & (from_y_ >= 0) & (from_y_ < ny)
            copy = pltpu.make_async_remote_copy(
                src_ref=raw.at[x_source, :, y_source],
                dst_ref=raw.at[x_target, :, y_target],
                send_sem=halo_send.at[slot, index],
                recv_sem=halo_recv.at[slot, index],
                device_id={"gx": lax.rem(to_x + nx, nx), "gy": lax.rem(to_y + ny, ny)},
                device_id_type=pl.DeviceIdType.MESH,
            )
            result.append((sends, receives, copy))
        return result

    def start(copies):
        for sends, _, copy in copies:
            pl.when(sends)(copy.start)

    def arrive(copies):
        for _, receives, copy in copies:
            pl.when(receives)(copy.wait_recv)

    def leave(copies):
        for sends, _, copy in copies:
            pl.when(sends)(copy.wait_send)

    place = lax.rem(lax.broadcasted_iota(jnp.int32, (CH, wide), 1), depth)
    first = place == 0
    last = place == depth - 1

    def shift(raw, out):
        def body(x, _):
            value = raw[x]
            out[x, CH : 2 * CH, :] = value
            full = value.astype(f32)
            out[x, :CH, :] = jnp.where(first, 0.0, pltpu.roll(full, 1, 1)).astype(bf16)
            out[x, 2 * CH :, :] = jnp.where(last, 0.0, pltpu.roll(full, wide - 1, 1)).astype(bf16)
            return 0

        lax.fori_loop(0, bx + 2, body, 0)

    def conv(field, weight, x):
        block = field[pl.ds(x, 3)].reshape(9 * CH, wide)
        taps = jnp.dot(weight[...], block, preferred_element_type=f32)
        return (
            taps[:CH, :lanes]
            + taps[CH : 2 * CH, depth : depth + lanes]
            + taps[2 * CH :, 2 * depth :]
        )

    def spread(out, x, value):
        for a in range(3):
            if a:
                out[x, a * CH : (a + 1) * CH, : a * depth] = jnp.zeros((CH, a * depth), bf16)
            if a < 2:
                out[x, a * CH : (a + 1) * CH, a * depth + lanes :] = jnp.zeros(
                    (CH, (2 - a) * depth), bf16
                )
            out[x, a * CH : (a + 1) * CH, a * depth : a * depth + lanes] = value

    def filter_grad(field, terms, slot):
        acc[...] = jnp.zeros_like(acc)

        def body(x, _):
            block = field[pl.ds(x, 3)].reshape(9 * CH, wide)
            acc[...] += lax.dot_general(
                block, terms[x], (((1,), (1,)), ((), ())), preferred_element_type=f32
            )
            return 0

        lax.fori_loop(0, bx, body, 0)
        used = 9 * CH
        mid = used // 2
        part[slot, :used, :] = acc[:, : 2 * CH].astype(bf16)
        part[slot, used : used + mid, :] = jnp.concatenate(
            [acc[:mid, 2 * CH :], acc[mid:, 2 * CH :]], axis=1
        ).astype(bf16)
        total = nx * ny * rows
        if total > used + mid:
            part[slot, used + mid :, :] = jnp.zeros((total - used - mid, 2 * CH), bf16)

    def remote(src, dst, send, recv, device):
        return pltpu.make_async_remote_copy(
            src_ref=src, dst_ref=dst, send_sem=send, recv_sem=recv,
            device_id=device, device_id_type=pl.DeviceIdType.MESH,
        )

    def span_x(index):
        return pl.ds(pl.multiple_of(index * (ny * rows), 16), ny * rows)

    def span_y(index):
        return pl.ds(pl.multiple_of(index * rows, 16), rows)

    def span_own(y):
        return pl.ds(pl.multiple_of((gx * ny + y) * rows, 16), rows)

    def scatter_x(slot):
        copies = []
        for d in range(1, nx):
            to = lax.rem(gx + d, nx)
            copies.append(remote(
                part.at[slot, span_x(to)], from_x.at[slot, d - 1],
                x_send.at[slot, d - 1], x_recv.at[slot, d - 1], {"gx": to},
            ))
            copies[-1].start()
        return copies

    def scatter_y(slot, copies):
        total = part[slot, span_x(gx)].astype(f32)
        for d, copy in enumerate(copies):
            copy.wait_recv()
            total = total + from_x[slot, d].astype(f32)
        half[slot] = total.astype(bf16)
        result = []
        for d in range(1, ny):
            to = lax.rem(gy + d, ny)
            result.append(remote(
                half.at[slot, span_y(to)], from_y.at[slot, d - 1],
                y_send.at[slot, d - 1], y_recv.at[slot, d - 1], {"gy": to},
            ))
            result[-1].start()
        return result

    def gather_y(slot, copies):
        total = half[slot, span_y(gy)].astype(f32)
        for d, copy in enumerate(copies):
            copy.wait_recv()
            total = total + from_y[slot, d].astype(f32)
        whole[slot, span_own(gy)] = total.astype(bf16)
        result = []
        for d in range(1, ny):
            to = lax.rem(gy + d, ny)
            result.append(remote(
                whole.at[slot, span_own(gy)], whole.at[slot, span_own(gy)],
                ay_send.at[slot, d - 1], ay_recv.at[slot, d - 1], {"gy": to},
            ))
            result[-1].start()
        return result

    def gather_x(slot, copies):
        for copy in copies:
            copy.wait_recv()
        result = []
        for d in range(1, nx):
            to = lax.rem(gx + d, nx)
            result.append(remote(
                whole.at[slot, span_x(gx)], whole.at[slot, span_x(gx)],
                ax_send.at[slot, d - 1], ax_recv.at[slot, d - 1], {"gx": to},
            ))
            result[-1].start()
        return result

    def finish(slot, copies, out):
        for copy in copies:
            copy.wait_recv()
        used = 9 * CH
        mid = used // 2
        both = whole[slot, :used, :].astype(f32)
        rest = whole[slot, used : used + mid, :].astype(f32)
        rest = jnp.concatenate([rest[:, :CH], rest[:, CH:]], axis=0)
        third = 3 * CH
        for a in range(3):
            out[a, 0] = both[a * third : (a + 1) * third, :CH]
            out[a, 1] = both[a * third : (a + 1) * third, CH:]
            out[a, 2] = rest[a * third : (a + 1) * third]

    in_copies = halo(raw_in, 0)
    start(in_copies)
    prepare()
    arrive(in_copies)
    shift(raw_in, sh_in)

    def first_layer(x, _):
        value = conv(sh_in, first_w, x)
        act[x] = value
        tangent = jnp.tanh(root_two_pi * (value + cubic_term * value * value * value))
        raw_hid[x + 1, :, inner] = (0.5 * value * (1.0 + tangent)).astype(bf16)
        return 0

    lax.fori_loop(0, bx, first_layer, 0)
    hid_copies = halo(raw_hid, 1)
    start(hid_copies)
    for b in range(3):
        back_w[b * CH : (b + 1) * CH, :] = turned(
            [w2_ref[((2 - a) * 3 + 2 - b) * 3 + 2 - c] for a in range(3) for c in range(3)]
        )

    def slopes(x, _):
        value = act[x]
        tangent = jnp.tanh(root_two_pi * (value + cubic_term * value * value * value))
        act[x] = 0.5 * (1.0 + tangent) + 0.5 * value * (
            1.0 - tangent * tangent
        ) * root_two_pi * (1.0 + 3.0 * cubic_term * value * value)
        return 0

    lax.fori_loop(0, bx, slopes, 0)
    arrive(hid_copies)
    shift(raw_hid, sh_hid)

    def second_layer(x, _):
        value = conv(sh_hid, second_w, x)
        pred_ref[x] = value.astype(bf16)
        grad = ((value - t_ref[x].astype(f32)) * normalizer).astype(bf16)
        raw_grad[x + 1, :, inner] = grad
        spread(wide_grad, x, grad)
        return 0

    lax.fori_loop(0, bx, second_layer, 0)
    grad_copies = halo(raw_grad, 2)
    start(grad_copies)
    filter_grad(sh_hid, wide_grad, 1)
    scatter_x_second = scatter_x(1)
    arrive(grad_copies)
    shift(raw_grad, sh_grad)

    def back(x, _):
        value = conv(sh_grad, back_w, x)
        spread(wide_slope, x, (value * act[x]).astype(bf16))
        return 0

    lax.fori_loop(0, bx, back, 0)
    scatter_y_second = scatter_y(1, scatter_x_second)
    filter_grad(sh_in, wide_slope, 0)
    scatter_x_first = scatter_x(0)
    gather_y_second = gather_y(1, scatter_y_second)
    scatter_y_first = scatter_y(0, scatter_x_first)
    gather_x_second = gather_x(1, gather_y_second)
    gather_y_first = gather_y(0, scatter_y_first)
    finish(1, gather_x_second, g2_ref)
    gather_x_first = gather_x(0, gather_y_first)
    finish(0, gather_x_first, g1_ref)

    for copies in (in_copies, hid_copies, grad_copies):
        leave(copies)
    for copies in (
        scatter_x_second, scatter_y_second, gather_y_second, gather_x_second,
        scatter_x_first, scatter_y_first, gather_y_first, gather_x_first,
    ):
        for copy in copies:
            copy.wait_send()


def on_device(nx, ny, inputs, target, w_first, w_second):
    bx, by, cin, depth = inputs.shape
    cout = target.shape[2]
    hid = w_first.shape[4]
    normalizer = 1.0 / math.sqrt(bx * nx * by * ny * depth)
    used = 9 * CH * 3 // 2
    rows = -(-used // (nx * ny * 16)) * 16

    def flat(field):
        rolled = field.transpose(0, 2, 1, 3).reshape(bx, field.shape[2], by * depth)
        return jnp.pad(rolled, ((0, 0), (0, CH - field.shape[2]), (0, 0)))

    def taps(w):
        return w.reshape((27,) + w.shape[3:])

    lanes = by * depth
    wide = lanes + 2 * depth
    vmem = pl.BlockSpec(memory_space=pltpu.VMEM)
    total = nx * ny * rows
    dma = pltpu.SemaphoreType.DMA
    macs = 5 * 192 * 576 * wide * bx
    prediction, g1, g2 = pl.pallas_call(
        functools.partial(kernel, nx, ny, bx, by, depth, rows, normalizer),
        out_shape=(
            jax.ShapeDtypeStruct((bx, CH, lanes), bf16),
            jax.ShapeDtypeStruct((3, 3, 3 * CH, CH), f32),
            jax.ShapeDtypeStruct((3, 3, 3 * CH, CH), f32),
        ),
        in_specs=[vmem] * 2 + [pl.BlockSpec(memory_space=pl.ANY)] * 2,
        out_specs=(vmem,) * 3,
        scratch_shapes=(
            [pltpu.VMEM((bx + 2, CH, wide), bf16)] * 3
            + [pltpu.VMEM((bx + 2, 3 * CH, wide), bf16)] * 3
            + [pltpu.VMEM((bx, 3 * CH, wide), bf16)] * 2
            + [pltpu.VMEM((27, cin, hid), bf16), pltpu.VMEM((27, cout, hid), bf16), dma((2,))]
            + [pltpu.VMEM((3 * CH, 9 * CH), bf16)] * 3
            + [
                pltpu.VMEM((bx, CH, lanes), f32),
                pltpu.VMEM((9 * CH, 3 * CH), f32),
                pltpu.VMEM((2, total, 2 * CH), bf16),
                pltpu.VMEM((2, nx - 1, ny * rows, 2 * CH), bf16),
                pltpu.VMEM((2, ny * rows, 2 * CH), bf16),
                pltpu.VMEM((2, ny - 1, rows, 2 * CH), bf16),
                pltpu.VMEM((2, total, 2 * CH), bf16),
                dma((3, 8)), dma((3, 8)),
                dma((2, nx - 1)), dma((2, nx - 1)),
                dma((2, ny - 1)), dma((2, ny - 1)),
                dma((2, ny - 1)), dma((2, ny - 1)),
                dma((2, nx - 1)), dma((2, nx - 1)),
            ]
        ),
        compiler_params=pltpu.CompilerParams(
            collective_id=0, has_side_effects=True, vmem_limit_bytes=48 * 1024 * 1024
        ),
        cost_estimate=pl.CostEstimate(
            flops=2 * macs, bytes_accessed=8 * 2**20, transcendentals=2 * bx * CH * lanes
        ),
    )(
        flat(inputs),
        flat(target),
        taps(w_first),
        taps(w_second.transpose(0, 1, 2, 4, 3)),
    )
    prediction = prediction.reshape(bx, CH, by, depth)[:, :cout].transpose(0, 2, 1, 3)
    g1 = g1.reshape(3, 3, 3, CH, CH)[:, :, :, :cin, :hid]
    g2 = g2.reshape(3, 3, 3, CH, CH)[:, :, :, :hid, :cout]
    return prediction, g1, g2


def solution(mesh):
    placed = (
        P(("groups", "gx"), "gy", None, None),
        P(("groups", "gx"), "gy", None, None),
        P(),
        P(),
    )
    return jax.shard_map(
        functools.partial(on_device, mesh.shape["gx"], mesh.shape["gy"]),
        mesh=mesh,
        in_specs=placed,
        out_specs=(
            P(("groups", "gx"), "gy", None, None),
            P("groups", None, None, None, None),
            P("groups", None, None, None, None),
        ),
        check_vma=False,
    )
```

```python
import functools
import math

import jax
import jax.numpy as jnp
from jax import lax
from jax.experimental import pallas as pl
from jax.experimental.pallas import tpu as pltpu
from jax.sharding import PartitionSpec as P

root_two_pi = 0.7978845608028654
cubic_term = 0.044715
CH = 64
bf16 = jnp.bfloat16
f32 = jnp.float32
DIRECTIONS = ((0, 1), (0, -1), (1, 0), (-1, 0), (1, 1), (1, -1), (-1, 1), (-1, -1))


def kernel(
    nx, ny, bx, by, depth, rows, normalizer,
    x_ref, t_ref, w1_hbm, w2_hbm,
    pred_ref, g1_ref, g2_ref,
    raw_in, raw_hid, raw_grad, sh_in, sh_hid, sh_grad, wide_grad, wide_slope,
    w1_ref, w2_ref, w_sem, first_w, second_w, back_w, act, acc, part, from_x, half, from_y, whole,
    halo_send, halo_recv, x_send, x_recv, y_send, y_recv, ay_send, ay_recv, ax_send, ax_recv,
):
    gx = lax.axis_index("gx")
    gy = lax.axis_index("gy")
    lanes = by * depth
    wide = lanes + 2 * depth
    inner = slice(depth, depth + lanes)

    loads = [
        pltpu.make_async_copy(w1_hbm, w1_ref, w_sem.at[0]),
        pltpu.make_async_copy(w2_hbm, w2_ref, w_sem.at[1]),
    ]
    for load in loads:
        load.start()
    for raw in (raw_in, raw_hid, raw_grad):
        raw[0] = jnp.zeros((CH, wide), bf16)
        raw[bx + 1] = jnp.zeros((CH, wide), bf16)
        raw[1 : bx + 1, :, :depth] = jnp.zeros((bx, CH, depth), bf16)
        raw[1 : bx + 1, :, depth + lanes :] = jnp.zeros((bx, CH, depth), bf16)
    raw_in[1 : bx + 1, :, inner] = x_ref[...]

    barrier = pltpu.get_barrier_semaphore()
    def filled(block):
        missing = CH - block.shape[0]
        return jnp.concatenate([block.astype(f32), jnp.zeros((missing, CH), f32)], axis=0)

    def turned(blocks):
        stacked = jnp.concatenate([filled(block) for block in blocks], axis=0)
        return stacked.T.astype(bf16)

    def prepare():
        for load in loads:
            load.wait()
        for b in range(3):
            first_w[b * CH : (b + 1) * CH, :] = turned(
                [w1_ref[(a * 3 + b) * 3 + c] for a in range(3) for c in range(3)]
            )
            for a in range(3):
                for c in range(3):
                    column = (a * 3 + c) * CH
                    second_w[b * CH : (b + 1) * CH, column : column + CH] = filled(
                        w2_ref[(a * 3 + b) * 3 + c]
                    ).astype(bf16)

    def greet(x, y):
        pl.semaphore_signal(
            barrier, inc=1, device_id={"gx": x, "gy": y}, device_id_type=pl.DeviceIdType.MESH
        )

    for dx, dy in DIRECTIONS[4:]:
        x, y = gx + dx, gy + dy
        pl.when((x >= 0) & (x < nx) & (y >= 0) & (y < ny))(
            functools.partial(greet, lax.rem(x + nx, nx), lax.rem(y + ny, ny))
        )
    for d in range(1, nx):
        greet(lax.rem(gx + d, nx), gy)
    for d in range(1, ny):
        greet(gx, lax.rem(gy + d, ny))
    beside_x = lax.div(gx + nx - 1, nx) + lax.div(2 * nx - 2 - gx, nx)
    beside_y = lax.div(gy + ny - 1, ny) + lax.div(2 * ny - 2 - gy, ny)
    pl.semaphore_wait(barrier, nx + ny - 2 + beside_x * beside_y)

    def spans(step, count, unit):
        source = {0: (1, count), 1: (count, 1), -1: (1, 1)}[step]
        target = {0: (1, count), 1: (0, 1), -1: (count + 1, 1)}[step]
        return (
            slice(source[0] * unit, (source[0] + source[1]) * unit),
            slice(target[0] * unit, (target[0] + target[1]) * unit),
        )

    def halo(raw, slot):
        result = []
        for index, (dx, dy) in enumerate(DIRECTIONS):
            x_source, x_target = spans(dx, bx, 1)
            y_source, y_target = spans(dy, by, depth)
            to_x, to_y = gx + dx, gy + dy
            from_x_, from_y_ = gx - dx, gy - dy
            sends = (to_x >= 0) & (to_x < nx) & (to_y >= 0) & (to_y < ny)
            receives = (from_x_ >= 0) & (from_x_ < nx) & (from_y_ >= 0) & (from_y_ < ny)
            copy = pltpu.make_async_remote_copy(
                src_ref=raw.at[x_source, :, y_source],
                dst_ref=raw.at[x_target, :, y_target],
                send_sem=halo_send.at[slot, index],
                recv_sem=halo_recv.at[slot, index],
                device_id={"gx": lax.rem(to_x + nx, nx), "gy": lax.rem(to_y + ny, ny)},
                device_id_type=pl.DeviceIdType.MESH,
            )
            result.append((sends, receives, copy))
        return result

    def start(copies):
        for sends, _, copy in copies:
            pl.when(sends)(copy.start)

    def arrive(copies):
        for _, receives, copy in copies:
            pl.when(receives)(copy.wait_recv)

    def leave(copies):
        for sends, _, copy in copies:
            pl.when(sends)(copy.wait_send)

    place = lax.rem(lax.broadcasted_iota(jnp.int32, (CH, wide), 1), depth)
    first = place == 0
    last = place == depth - 1

    def shift(raw, out):
        def body(x, _):
            value = raw[x]
            out[x, CH : 2 * CH, :] = value
            full = value.astype(f32)
            out[x, :CH, :] = jnp.where(first, 0.0, pltpu.roll(full, 1, 1)).astype(bf16)
            out[x, 2 * CH :, :] = jnp.where(last, 0.0, pltpu.roll(full, wide - 1, 1)).astype(bf16)
            return 0

        lax.fori_loop(0, bx + 2, body, 0)

    def conv(field, weight, x):
        block = field[pl.ds(x, 3)].reshape(9 * CH, wide)
        taps = jnp.dot(weight[...], block, preferred_element_type=f32)
        return (
            taps[:CH, :lanes]
            + taps[CH : 2 * CH, depth : depth + lanes]
            + taps[2 * CH :, 2 * depth :]
        )

    def spread(out, x, value):
        for a in range(3):
            if a:
                out[x, a * CH : (a + 1) * CH, : a * depth] = jnp.zeros((CH, a * depth), bf16)
            if a < 2:
                out[x, a * CH : (a + 1) * CH, a * depth + lanes :] = jnp.zeros(
                    (CH, (2 - a) * depth), bf16
                )
            out[x, a * CH : (a + 1) * CH, a * depth : a * depth + lanes] = value

    def filter_grad(field, terms, slot):
        acc[...] = jnp.zeros_like(acc)

        def body(x, _):
            block = field[pl.ds(x, 3)].reshape(9 * CH, wide)
            acc[...] += lax.dot_general(
                block, terms[x], (((1,), (1,)), ((), ())), preferred_element_type=f32
            )
            return 0

        lax.fori_loop(0, bx, body, 0, unroll=True)
        used = 9 * CH
        mid = used // 2
        part[slot, :used, :] = acc[:, : 2 * CH].astype(bf16)
        part[slot, used : used + mid, :] = jnp.concatenate(
            [acc[:mid, 2 * CH :], acc[mid:, 2 * CH :]], axis=1
        ).astype(bf16)
        total = nx * ny * rows
        if total > used + mid:
            part[slot, used + mid :, :] = jnp.zeros((total - used - mid, 2 * CH), bf16)

    def remote(src, dst, send, recv, device):
        return pltpu.make_async_remote_copy(
            src_ref=src, dst_ref=dst, send_sem=send, recv_sem=recv,
            device_id=device, device_id_type=pl.DeviceIdType.MESH,
        )

    def span_x(index):
        return pl.ds(pl.multiple_of(index * (ny * rows), 16), ny * rows)

    def span_y(index):
        return pl.ds(pl.multiple_of(index * rows, 16), rows)

    def span_own(y):
        return pl.ds(pl.multiple_of((gx * ny + y) * rows, 16), rows)

    def scatter_x(slot):
        copies = []
        for d in range(1, nx):
            to = lax.rem(gx + d, nx)
            copies.append(remote(
                part.at[slot, span_x(to)], from_x.at[slot, d - 1],
                x_send.at[slot, d - 1], x_recv.at[slot, d - 1], {"gx": to},
            ))
            copies[-1].start()
        return copies

    def scatter_y(slot, copies):
        total = part[slot, span_x(gx)].astype(f32)
        for d, copy in enumerate(copies):
            copy.wait_recv()
            total = total + from_x[slot, d].astype(f32)
        half[slot] = total.astype(bf16)
        result = []
        for d in range(1, ny):
            to = lax.rem(gy + d, ny)
            result.append(remote(
                half.at[slot, span_y(to)], from_y.at[slot, d - 1],
                y_send.at[slot, d - 1], y_recv.at[slot, d - 1], {"gy": to},
            ))
            result[-1].start()
        return result

    def gather_y(slot, copies):
        total = half[slot, span_y(gy)].astype(f32)
        for d, copy in enumerate(copies):
            copy.wait_recv()
            total = total + from_y[slot, d].astype(f32)
        whole[slot, span_own(gy)] = total.astype(bf16)
        result = []
        for d in range(1, ny):
            to = lax.rem(gy + d, ny)
            result.append(remote(
                whole.at[slot, span_own(gy)], whole.at[slot, span_own(gy)],
                ay_send.at[slot, d - 1], ay_recv.at[slot, d - 1], {"gy": to},
            ))
            result[-1].start()
        return result

    def gather_x(slot, copies):
        for copy in copies:
            copy.wait_recv()
        result = []
        for d in range(1, nx):
            to = lax.rem(gx + d, nx)
            result.append(remote(
                whole.at[slot, span_x(gx)], whole.at[slot, span_x(gx)],
                ax_send.at[slot, d - 1], ax_recv.at[slot, d - 1], {"gx": to},
            ))
            result[-1].start()
        return result

    def finish(slot, copies, out):
        for copy in copies:
            copy.wait_recv()
        used = 9 * CH
        mid = used // 2
        both = whole[slot, :used, :].astype(f32)
        rest = whole[slot, used : used + mid, :].astype(f32)
        rest = jnp.concatenate([rest[:, :CH], rest[:, CH:]], axis=0)
        third = 3 * CH
        for a in range(3):
            out[a, 0] = both[a * third : (a + 1) * third, :CH]
            out[a, 1] = both[a * third : (a + 1) * third, CH:]
            out[a, 2] = rest[a * third : (a + 1) * third]

    in_copies = halo(raw_in, 0)
    start(in_copies)
    prepare()
    arrive(in_copies)
    shift(raw_in, sh_in)

    def first_layer(x, _):
        value = conv(sh_in, first_w, x)
        act[x] = value
        tangent = jnp.tanh(root_two_pi * (value + cubic_term * value * value * value))
        raw_hid[x + 1, :, inner] = (0.5 * value * (1.0 + tangent)).astype(bf16)
        return 0

    lax.fori_loop(0, bx, first_layer, 0, unroll=True)
    hid_copies = halo(raw_hid, 1)
    start(hid_copies)
    for b in range(3):
        back_w[b * CH : (b + 1) * CH, :] = turned(
            [w2_ref[((2 - a) * 3 + 2 - b) * 3 + 2 - c] for a in range(3) for c in range(3)]
        )

    def slopes(x, _):
        value = act[x]
        tangent = jnp.tanh(root_two_pi * (value + cubic_term * value * value * value))
        act[x] = 0.5 * (1.0 + tangent) + 0.5 * value * (
            1.0 - tangent * tangent
        ) * root_two_pi * (1.0 + 3.0 * cubic_term * value * value)
        return 0

    lax.fori_loop(0, bx, slopes, 0, unroll=True)
    arrive(hid_copies)
    shift(raw_hid, sh_hid)

    def second_layer(x, _):
        value = conv(sh_hid, second_w, x)
        pred_ref[x] = value.astype(bf16)
        grad = ((value - t_ref[x].astype(f32)) * normalizer).astype(bf16)
        raw_grad[x + 1, :, inner] = grad
        spread(wide_grad, x, grad)
        return 0

    lax.fori_loop(0, bx, second_layer, 0, unroll=True)
    grad_copies = halo(raw_grad, 2)
    start(grad_copies)
    filter_grad(sh_hid, wide_grad, 1)
    scatter_x_second = scatter_x(1)
    arrive(grad_copies)
    shift(raw_grad, sh_grad)

    def back(x, _):
        value = conv(sh_grad, back_w, x)
        spread(wide_slope, x, (value * act[x]).astype(bf16))
        return 0

    lax.fori_loop(0, bx, back, 0, unroll=True)
    scatter_y_second = scatter_y(1, scatter_x_second)
    filter_grad(sh_in, wide_slope, 0)
    scatter_x_first = scatter_x(0)
    gather_y_second = gather_y(1, scatter_y_second)
    scatter_y_first = scatter_y(0, scatter_x_first)
    gather_x_second = gather_x(1, gather_y_second)
    gather_y_first = gather_y(0, scatter_y_first)
    finish(1, gather_x_second, g2_ref)
    gather_x_first = gather_x(0, gather_y_first)
    finish(0, gather_x_first, g1_ref)

    for copies in (in_copies, hid_copies, grad_copies):
        leave(copies)
    for copies in (
        scatter_x_second, scatter_y_second, gather_y_second, gather_x_second,
        scatter_x_first, scatter_y_first, gather_y_first, gather_x_first,
    ):
        for copy in copies:
            copy.wait_send()


def on_device(nx, ny, inputs, target, w_first, w_second):
    bx, by, cin, depth = inputs.shape
    cout = target.shape[2]
    hid = w_first.shape[4]
    normalizer = 1.0 / math.sqrt(bx * nx * by * ny * depth)
    used = 9 * CH * 3 // 2
    rows = -(-used // (nx * ny * 16)) * 16

    def flat(field):
        rolled = field.transpose(0, 2, 1, 3).reshape(bx, field.shape[2], by * depth)
        return jnp.pad(rolled, ((0, 0), (0, CH - field.shape[2]), (0, 0)))

    def taps(w):
        return w.reshape((27,) + w.shape[3:])

    lanes = by * depth
    wide = lanes + 2 * depth
    vmem = pl.BlockSpec(memory_space=pltpu.VMEM)
    total = nx * ny * rows
    dma = pltpu.SemaphoreType.DMA
    macs = 5 * 192 * 576 * wide * bx
    prediction, g1, g2 = pl.pallas_call(
        functools.partial(kernel, nx, ny, bx, by, depth, rows, normalizer),
        out_shape=(
            jax.ShapeDtypeStruct((bx, CH, lanes), bf16),
            jax.ShapeDtypeStruct((3, 3, 3 * CH, CH), f32),
            jax.ShapeDtypeStruct((3, 3, 3 * CH, CH), f32),
        ),
        in_specs=[vmem] * 2 + [pl.BlockSpec(memory_space=pl.ANY)] * 2,
        out_specs=(vmem,) * 3,
        scratch_shapes=(
            [pltpu.VMEM((bx + 2, CH, wide), bf16)] * 3
            + [pltpu.VMEM((bx + 2, 3 * CH, wide), bf16)] * 3
            + [pltpu.VMEM((bx, 3 * CH, wide), bf16)] * 2
            + [pltpu.VMEM((27, cin, hid), bf16), pltpu.VMEM((27, cout, hid), bf16), dma((2,))]
            + [pltpu.VMEM((3 * CH, 9 * CH), bf16)] * 3
            + [
                pltpu.VMEM((bx, CH, lanes), f32),
                pltpu.VMEM((9 * CH, 3 * CH), f32),
                pltpu.VMEM((2, total, 2 * CH), bf16),
                pltpu.VMEM((2, nx - 1, ny * rows, 2 * CH), bf16),
                pltpu.VMEM((2, ny * rows, 2 * CH), bf16),
                pltpu.VMEM((2, ny - 1, rows, 2 * CH), bf16),
                pltpu.VMEM((2, total, 2 * CH), bf16),
                dma((3, 8)), dma((3, 8)),
                dma((2, nx - 1)), dma((2, nx - 1)),
                dma((2, ny - 1)), dma((2, ny - 1)),
                dma((2, ny - 1)), dma((2, ny - 1)),
                dma((2, nx - 1)), dma((2, nx - 1)),
            ]
        ),
        compiler_params=pltpu.CompilerParams(
            collective_id=0, has_side_effects=True, vmem_limit_bytes=48 * 1024 * 1024
        ),
        cost_estimate=pl.CostEstimate(
            flops=2 * macs, bytes_accessed=8 * 2**20, transcendentals=2 * bx * CH * lanes
        ),
    )(
        flat(inputs),
        flat(target),
        taps(w_first),
        taps(w_second.transpose(0, 1, 2, 4, 3)),
    )
    prediction = prediction.reshape(bx, CH, by, depth)[:, :cout].transpose(0, 2, 1, 3)
    g1 = g1.reshape(3, 3, 3, CH, CH)[:, :, :, :cin, :hid]
    g2 = g2.reshape(3, 3, 3, CH, CH)[:, :, :, :hid, :cout]
    return prediction, g1, g2


def solution(mesh):
    placed = (
        P(("groups", "gx"), "gy", None, None),
        P(("groups", "gx"), "gy", None, None),
        P(),
        P(),
    )
    return jax.shard_map(
        functools.partial(on_device, mesh.shape["gx"], mesh.shape["gy"]),
        mesh=mesh,
        in_specs=placed,
        out_specs=(
            P(("groups", "gx"), "gy", None, None),
            P("groups", None, None, None, None),
            P("groups", None, None, None, None),
        ),
        check_vma=False,
    )
```
